32 devices in a mesh: sec: 16 (over z, x, core), env: 2 (over y).
Axes of the slice: x: 2, y: 2, z: 4, core: 2. Of those that a mesh axis runs over, the one named last changes fastest.
Arguments:
- left_env: bfloat16 [1024, 10, 1024], P('sec'), may hold values from -0.1875 to 0.1875
- left_site: bfloat16 [16384, 4, 1024], P('sec', None, 'env'), may hold values from -6 to 6
- bond_vec: float32 [16384], P(('sec', 'env')), may hold values from 0.25 to 4
- right_site: bfloat16 [16384, 4, 1024], P('sec', None, 'env'), may hold values from -0.1875 to 0.1875
- right_env: bfloat16 [16384, 10, 1024], P('sec', None, 'env'), may hold values from -0.0625 to 0.0625
- mpo: float32 [200, 1600], replicated, may hold values from -1 to 1
- bond_profile: int32 [200], replicated, may hold values from 256 to 1024, as said below
- lengths: int32 [16], P('sec'), may hold values from 1 to 16, 200 in all
Outputs:
- junction_out: bfloat16 [1024, 4, 4, 1024], P('sec')
The draws below stay inside these ranges and needn't reach their ends.
Inputs may be any that keep to these rules, and one draw needn't show every extreme that they name: `bond_profile`: every entry is at least 256 and at most 1024; both ends are taken in every draw. The lengths sum to 200; the longest section has exactly 16 sites.
All inputs are finite; a program needn't handle non-finite values. No bound on the sum of `lengths` on one device may be relied on, other than what follows from the above.
Results may differ from the reference program's by a relative error of at most 0.007.
Values may be sent and summed in bfloat16 or wider, within the bound.
A program may use at most 128 MiB of HBM per device.

```python
import math
import jax
import jax.numpy as jnp
import numpy as np
from jax import lax

CHI = 1024
W = 10
DL = 4
SITES = 200
MOST_LEN = 16
ROWS = 64
N_SEC = 16


def draw_bond_profile(key, part):
    key = jax.random.fold_in(key, 7)
    first_key, second_key = jax.random.split(key)
    values = jax.random.randint(first_key, (SITES,), CHI // 4, CHI + 1)
    spots = jax.random.permutation(second_key, SITES)
    values = values.at[spots[0]].set(CHI)
    values = values.at[spots[1]].set(CHI // 4)
    return values.astype(jnp.int32)


def block_scale(key, dims, cuts, smallest, top_value):
    gain, own = 1.0, jax.random.fold_in(key, 6)
    for axis_at, blocks in cuts:
        steps = jnp.exp(jax.random.uniform(jax.random.fold_in(own, axis_at), (blocks,), jnp.float32, smallest / len(cuts), top_value / len(cuts)))
        gain = gain * jnp.repeat(steps, dims[axis_at] // blocks).reshape([-1 if axis == axis_at else 1 for axis in range(len(dims))])
    return gain


def length_profile(number_of, total, bound, skew):
    loads = [(1 << 20) // math.isqrt(standing ** skew) + 1 for standing in range(2, number_of + 1)]
    surplus, counts = total - bound - (number_of - 1), [1] * (number_of - 1)
    while surplus > 0:
        movable = [i for i in range(number_of - 1) if counts[i] < bound]
        mass, budget = sum([loads[i] for i in movable]), surplus
        for i in movable:
            extra = min(bound - counts[i], max(1, budget * loads[i] // mass), surplus)
            counts[i] = counts[i] + extra
            surplus = surplus - extra
    return np.array([bound] + counts)


def ragged_sizes(rng, amount, total, bound, lean):
    if amount == 2:
        one = jax.random.randint(rng, (), max(1, total - bound), min(bound, total - 1) + 1)
        return jnp.stack([one, total - one])
    sizes = jnp.asarray(length_profile(amount, total, bound, lean), jnp.int32)
    couples = (amount - 1) // 2
    donor, receiver = sizes[1:1 + 2 * couples:2], sizes[2:2 + 2 * couples:2]
    margin = jnp.minimum(donor - 1, bound - receiver)
    shifted = jax.random.randint(jax.random.fold_in(rng, 1), (couples,), 0, 1 << 20) % (margin + 1)
    sizes = sizes.at[1:1 + 2 * couples:2].set(donor - shifted).at[2:2 + 2 * couples:2].set(receiver + shifted)
    return sizes[jax.random.permutation(jax.random.fold_in(rng, 2), amount)]


def gaussian(stream_key, dims, scale, bound, cuts=(), kind=jnp.bfloat16):
    entries = jax.random.normal(stream_key, dims, jnp.float32) * scale
    if len(cuts) > 0:
        entries = block_scale(stream_key, dims, cuts, -0.22, 0.18) * entries
    return jnp.clip(entries, min=-bound, max=bound).astype(kind)


def setup_inputs(seed: int = 0) -> dict:
    keys = jax.random.split(jax.random.key(seed), 9)
    return {
        "left_env": gaussian(keys[0], (N_SEC * ROWS, W, CHI), CHI ** -0.5, 0.1875, ((0, 16),)),
        "left_site": gaussian(keys[1], (N_SEC * CHI, DL, CHI), 1.0, 6.0, ((0, 16), (2, 2))),
        "bond_vec": jnp.clip(jnp.exp(math.log(4.0) - 2.7725887 * jax.random.uniform(keys[2], (N_SEC * CHI,), jnp.float32) ** block_scale(keys[2], (N_SEC * CHI,), ((0, 32),), -0.2, 0.2)), 0.25, 4.0),
        "right_site": gaussian(keys[3], (N_SEC * CHI, DL, CHI), CHI ** -0.5, 0.1875, ((0, 16), (2, 2))),
        "right_env": gaussian(keys[4], (N_SEC * CHI, W, CHI), (W * CHI) ** -0.5, 0.0625, ((0, 16), (2, 2))),
        "mpo": gaussian(keys[5], (SITES, W * W * DL * DL), (W * DL) ** -0.5, 1.0, (), jnp.float32),
        "bond_profile": draw_bond_profile(jax.random.fold_in(keys[8], 71), 0),
        "lengths": ragged_sizes(keys[7], N_SEC, SITES, MOST_LEN, 2).astype(jnp.int32),
    }


def reference(left_env, left_site, bond_vec, right_site, right_env, mpo, bond_profile, lengths):
    high = lax.Precision.HIGHEST
    ends = (jnp.cumsum(lengths) - 1).astype(jnp.int32)
    tables = mpo.reshape(SITES, W, W, DL, DL)
    bond_ids = jnp.arange(CHI, dtype=jnp.int32)

    def junction(index):
        own_site = ends[index]
        before_site = ((own_site - 1) % SITES).astype(jnp.int32)
        after_site = ((own_site + 1) % SITES).astype(jnp.int32)
        left_live = bond_profile[before_site]
        middle_live = bond_profile[own_site]
        right_live = bond_profile[after_site]
        following = ((index + 1) % N_SEC).astype(jnp.int32)
        env_rows = lax.dynamic_slice_in_dim(left_env, (index * ROWS).astype(jnp.int32), ROWS, 0)
        left_block = lax.dynamic_slice_in_dim(left_site, (index * CHI).astype(jnp.int32), CHI, 0)
        weights = lax.dynamic_slice_in_dim(bond_vec, (index * CHI).astype(jnp.int32), CHI, 0)
        site_next = lax.dynamic_slice_in_dim(right_site, (following * CHI).astype(jnp.int32), CHI, 0)
        env_next = lax.dynamic_slice_in_dim(right_env, (following * CHI).astype(jnp.int32), CHI, 0)
        keep_left = (bond_ids < left_live)[:, None, None] & (bond_ids < middle_live)[None, None, :]
        left_used = jnp.where(keep_left, left_block.astype(jnp.float32), 0.0)
        row_block = jnp.einsum("xmy,yuc->xmuc", env_rows.astype(jnp.float32), left_used, precision=high)
        row_block = (row_block * weights[None, None, None, :]).astype(jnp.bfloat16)
        site_used = jnp.where((bond_ids < right_live)[None, None, :], site_next.astype(jnp.float32), 0.0)
        inner = jnp.einsum("xmuc,cvb->xmuvb", row_block.astype(jnp.float32), site_used, precision=high)
        inner = inner.astype(jnp.bfloat16)
        first_table = tables[own_site]
        second_table = tables[after_site]
        mpo_pair = jnp.einsum("mnsu,nktv->msuktv", first_table, second_table, precision=high).astype(jnp.bfloat16)
        mixed = jnp.einsum("xmuvb,msuktv->xstkb", inner.astype(jnp.float32), mpo_pair.astype(jnp.float32), precision=high)
        mixed = mixed.astype(jnp.bfloat16)
        env_used = jnp.where((bond_ids < right_live)[:, None, None], env_next.astype(jnp.float32), 0.0)
        result = jnp.einsum("xstkf,bkf->xstb", mixed.astype(jnp.float32), env_used, precision=high)
        return result.astype(jnp.bfloat16)

    outputs = lax.map(junction, jnp.arange(N_SEC, dtype=jnp.int32))
    return outputs.reshape(N_SEC * ROWS, DL, DL, CHI)
```

```python
import functools

import jax
import jax.numpy as jnp
from jax import lax
from jax.experimental import pallas as pl
from jax.experimental.pallas import tpu as pltpu
from jax.sharding import PartitionSpec as P

CHUNKS = 2
GROUP = 8
VMEM_BYTES = 56 * 1024 * 1024


def row_kernel(env_ref, site_ref, scale_ref, out_ref, held):
    state = pl.program_id(0)
    states = pl.num_programs(0)
    rows = env_ref.shape[0]
    part = jnp.dot(env_ref[...], site_ref[0], preferred_element_type=jnp.float32)
    part = part * scale_ref[...]
    for u in range(out_ref.shape[0] // rows):

        @pl.when(state == u)
        def _():
            for at in range(0, part.shape[1], 128):
                held[at // 128, pl.ds(u, rows, stride=out_ref.shape[0] // rows), :] = part[:, at:at + 128]

    @pl.when(state == states - 1)
    def _():
        for at in range(held.shape[0]):
            out_ref[:, at * 128:(at + 1) * 128] = held[at].astype(out_ref.dtype)


def make_rows(env_rows, left_site, scale):
    rows, depth = env_rows.shape
    states, _, width = left_site.shape
    return pl.pallas_call(
        row_kernel,
        grid=(states,),
        in_specs=[
            pl.BlockSpec((rows, depth), lambda u: (0, 0)),
            pl.BlockSpec((1, depth, width), lambda u: (u, 0, 0)),
            pl.BlockSpec((1, width), lambda u: (0, 0)),
        ],
        out_specs=pl.BlockSpec((rows * states, width), lambda u: (0, 0)),
        out_shape=jax.ShapeDtypeStruct((rows * states, width), jnp.bfloat16),
        scratch_shapes=[pltpu.VMEM((width // 128, rows * states, 128), jnp.float32)],
        compiler_params=pltpu.CompilerParams(vmem_limit_bytes=VMEM_BYTES),
        cost_estimate=pl.CostEstimate(
            flops=2 * rows * states * depth * width,
            bytes_accessed=2 * (rows * depth + states * depth * width + rows * states * width),
            transcendentals=0,
        ),
    )(env_rows, left_site, scale)


def apply_kernel(pieces, *refs):
    rows_refs = refs[:pieces]
    site_ref, env_ref, pair_ref, mask_ref, out_ref, mixed, total = refs[pieces:]
    step = pl.program_id(0)
    last = pl.num_programs(0) - 1
    place = lax.axis_index("env")
    states, _, width = site_ref.shape
    block = rows_refs[0].shape[1]
    bonds = mixed.shape[0]
    pairs = pair_ref.shape[0] // bonds
    tall = pair_ref.shape[1] // states

    @pl.when(step == 0)
    def _():
        def group(g, carry):
            base = pl.multiple_of(g * (GROUP * tall), 16)
            parts = []
            for v in range(states):
                term = None
                for r in range(pieces):
                    at = pl.multiple_of(lax.rem(place - r + pieces, pieces) * block, 128)
                    one = jnp.dot(
                        rows_refs[r][pl.ds(base, GROUP * tall), :],
                        site_ref[v, pl.ds(at, block), :],
                        preferred_element_type=jnp.float32,
                    )
                    term = one if term is None else term + one
                parts.append(term * mask_ref[...])
            for i in range(GROUP):
                inner = jnp.concatenate([p[i * tall:(i + 1) * tall] for p in parts], axis=0)
                out = jnp.dot(pair_ref[...], inner.astype(jnp.bfloat16), preferred_element_type=jnp.float32)
                out = out.astype(jnp.bfloat16)
                start = pl.multiple_of((g * GROUP + i) * pairs, 16)
                for k in range(bonds):
                    mixed[k, pl.ds(start, pairs), :] = out[k * pairs:(k + 1) * pairs]
            return carry

        lax.fori_loop(0, mixed.shape[1] // (GROUP * pairs), group, 0)
        total[...] = jnp.zeros_like(total)

    total[...] += lax.dot_general(
        mixed[step], env_ref[0], (((1,), (1,)), ((), ())), preferred_element_type=jnp.float32
    )

    @pl.when(step == last)
    def _():
        out_ref[...] = total[...].astype(out_ref.dtype)


def make_terms(rows_pieces, site, env, pair, mask):
    pieces = len(rows_pieces)
    count, block = rows_pieces[0].shape
    states, depth, width = site.shape
    bonds, outs, _ = env.shape
    tall = bonds * states
    lines = count // tall * states * states
    whole = lambda k: (0, 0)
    return pl.pallas_call(
        functools.partial(apply_kernel, pieces),
        grid=(bonds,),
        in_specs=[pl.BlockSpec((count, block), whole)] * pieces
        + [
            pl.BlockSpec((states, depth, width), lambda k: (0, 0, 0)),
            pl.BlockSpec((1, outs, width), lambda k: (k, 0, 0)),
            pl.BlockSpec(pair.shape, whole),
            pl.BlockSpec(mask.shape, whole),
        ],
        out_specs=pl.BlockSpec((lines, outs), whole),
        out_shape=jax.ShapeDtypeStruct((lines, outs), jnp.bfloat16),
        scratch_shapes=[
            pltpu.VMEM((bonds, lines, width), jnp.bfloat16),
            pltpu.VMEM((lines, outs), jnp.float32),
        ],
        compiler_params=pltpu.CompilerParams(vmem_limit_bytes=VMEM_BYTES),
        cost_estimate=pl.CostEstimate(
            flops=4 * count * depth * states * width + 2 * lines * outs * width * bonds,
            bytes_accessed=2 * (states * depth * width + bonds * outs * width + count * depth + lines * outs),
            transcendentals=0,
        ),
    )(*rows_pieces, site, env, pair, mask)


def hop(value, sections, blocks, sec_step, env_step):
    pairs = [
        (s * blocks + e, (s + sec_step) % sections * blocks + (e + env_step) % blocks)
        for s in range(sections)
        for e in range(blocks)
    ]
    return lax.ppermute(value, ("sec", "env"), pairs)


def body(left_env, left_site, bond_vec, right_site, right_env, mpo, bond_profile, lengths):
    sections, blocks = lax.axis_size("sec"), lax.axis_size("env")
    rows, bonds, width = left_env.shape
    _, states, block = left_site.shape
    sites = mpo.shape[0]
    here = lax.axis_index("sec")
    columns = lax.axis_index("env") * block + jnp.arange(block, dtype=jnp.int32)
    ids = jnp.arange(width, dtype=jnp.int32)

    all_lengths = lax.all_gather(lengths, "sec", tiled=True)
    start = jnp.sum(jnp.where(jnp.arange(sections) < here, all_lengths, 0))
    own = start + lengths[0] - 1
    left_live = bond_profile[(own - 1) % sites]
    middle_live = bond_profile[own % sites]
    out_live = bond_profile[(own + 1) % sites]
    before = (start - 1) % sites
    first = start % sites
    right_live = bond_profile[first]

    left_used = jnp.transpose(left_site, (1, 0, 2))
    env_rows = jnp.where((ids < left_live)[None, None, :], left_env, jnp.zeros_like(left_env))
    env_rows = env_rows.reshape(rows * bonds, width)
    scale = jnp.where(columns < middle_live, bond_vec, 0.0)[None, :]

    step = rows // CHUNKS
    sent = []
    for chunk in range(CHUNKS):
        part = make_rows(env_rows[chunk * step * bonds:(chunk + 1) * step * bonds], left_used, scale)
        sent.append([hop(part, sections, blocks, 1, r) for r in range(blocks)])

    site = jnp.transpose(right_site, (1, 0, 2))
    env = jnp.transpose(right_env, (1, 0, 2))
    mask = (columns < right_live).astype(jnp.float32)[None, :]
    tables = mpo.reshape(sites, -1)
    one = lax.dynamic_index_in_dim(tables, before, 0, False).reshape(bonds, bonds, states, states)
    two = lax.dynamic_index_in_dim(tables, first, 0, False).reshape(bonds, bonds, states, states)
    pair = jnp.einsum("mnsu,nktv->kstvmu", one, two, precision=lax.Precision.HIGHEST)
    pair = pair.reshape(bonds * states * states, -1).astype(jnp.bfloat16)

    keep = (ids < out_live)[None, :]
    results = []
    for chunk in range(CHUNKS):
        terms = make_terms(sent[chunk], site, env, pair, mask)
        back = [hop(terms, sections, blocks, -1, r) for r in range(blocks)]
        total = sum(b.astype(jnp.float32) for b in back)
        results.append(jnp.where(keep, total, 0.0).astype(jnp.bfloat16))
    return jnp.concatenate(results, axis=0).reshape(rows, states, states, width)


def solution(mesh):
    return jax.shard_map(
        body,
        mesh=mesh,
        in_specs=(
            P("sec", None, None),
            P("sec", None, "env"),
            P(("sec", "env")),
            P("sec", None, "env"),
            P("sec", None, "env"),
            P(),
            P(),
            P("sec"),
        ),
        out_specs=P("sec", None, None, None),
        check_vma=False,
    )
```

```python
import functools

import jax
import jax.numpy as jnp
from jax import lax
from jax.experimental import pallas as pl
from jax.experimental.pallas import tpu as pltpu
from jax.sharding import PartitionSpec as P

CHUNK_PARTS = (1, 2, 1)
GROUP = 8
VMEM_BYTES = 56 * 1024 * 1024


def count_kernel(length_ref, start_ref, slots, send_sem, recv_sem):
    sections = slots.shape[0]
    me = lax.axis_index("sec")
    barrier = pltpu.get_barrier_semaphore()
    for off in range(1, sections):
        pl.semaphore_signal(
            barrier,
            inc=1,
            device_id={"sec": lax.rem(me + off, sections)},
            device_id_type=pl.DeviceIdType.MESH,
        )
    pl.semaphore_wait(barrier, sections - 1)
    copies = []
    for off in range(1, sections):
        copy = pltpu.make_async_remote_copy(
            src_ref=length_ref,
            dst_ref=slots.at[off],
            send_sem=send_sem.at[off],
            recv_sem=recv_sem.at[off],
            device_id={"sec": lax.rem(me + off, sections)},
            device_id_type=pl.DeviceIdType.MESH,
        )
        copy.start()
        copies.append(copy)
    for copy in copies:
        copy.wait()
    total = jnp.zeros_like(start_ref)
    for off in range(1, sections):
        total = total + slots[off] * (me >= off).astype(jnp.int32)
    start_ref[...] = total


def earlier_sites(lengths, sections):
    tile = (8, 128)
    start = pl.pallas_call(
        count_kernel,
        in_specs=[pl.BlockSpec(memory_space=pltpu.VMEM)],
        out_specs=pl.BlockSpec(memory_space=pltpu.VMEM),
        out_shape=jax.ShapeDtypeStruct(tile, jnp.int32),
        scratch_shapes=[
            pltpu.VMEM((sections,) + tile, jnp.int32),
            pltpu.SemaphoreType.DMA((sections,)),
            pltpu.SemaphoreType.DMA((sections,)),
        ],
        compiler_params=pltpu.CompilerParams(collective_id=0, has_side_effects=True),
    )(jnp.broadcast_to(lengths[None, :], tile))
    return start[0, 0]


def row_kernel(live_ref, env_ref, site_ref, weight_ref, out_ref, used, held):
    state = pl.program_id(0)
    states = pl.num_programs(0)
    rows, depth = env_ref.shape
    width = weight_ref.shape[1]
    count = out_ref.shape[0] // rows

    @pl.when(state == 0)
    def _():
        ids = lax.broadcasted_iota(jnp.int32, (1, depth), 1)
        keep = (ids < live_ref[0]).astype(jnp.float32).astype(jnp.bfloat16)
        used[...] = env_ref[...] * keep

    ids = lax.axis_index("env") * width + lax.broadcasted_iota(jnp.int32, (1, width), 1)
    scale = jnp.where(ids < live_ref[1], weight_ref[...], 0.0)
    part = jnp.dot(used[...], site_ref[0], preferred_element_type=jnp.float32) * scale
    for u in range(count):

        @pl.when(state == u)
        def _():
            for at in range(held.shape[0]):
                held[at, pl.ds(u, rows, stride=count), :] = part[:, at * 128:(at + 1) * 128]

    @pl.when(state == states - 1)
    def _():
        for at in range(held.shape[0]):
            out_ref[:, at * 128:(at + 1) * 128] = held[at].astype(out_ref.dtype)


def make_rows(live, env_rows, left_site, weights):
    rows, depth = env_rows.shape
    states, _, width = left_site.shape
    return pl.pallas_call(
        row_kernel,
        grid=(states,),
        in_specs=[
            pl.BlockSpec(memory_space=pltpu.SMEM),
            pl.BlockSpec((rows, depth), lambda u: (0, 0)),
            pl.BlockSpec((1, depth, width), lambda u: (u, 0, 0)),
            pl.BlockSpec((1, width), lambda u: (0, 0)),
        ],
        out_specs=pl.BlockSpec((rows * states, width), lambda u: (0, 0)),
        out_shape=jax.ShapeDtypeStruct((rows * states, width), jnp.bfloat16),
        scratch_shapes=[
            pltpu.VMEM((rows, depth), jnp.bfloat16),
            pltpu.VMEM((width // 128, rows * states, 128), jnp.float32),
        ],
        compiler_params=pltpu.CompilerParams(vmem_limit_bytes=VMEM_BYTES),
        cost_estimate=pl.CostEstimate(
            flops=2 * rows * states * depth * width,
            bytes_accessed=2 * (rows * depth + states * depth * width + rows * states * width),
            transcendentals=0,
        ),
    )(live, env_rows, left_site, weights)


def apply_kernel(pieces, *refs):
    rows_refs = refs[:pieces]
    site_ref, env_ref, pair_ref, mask_ref, out_ref, mixed, total = refs[pieces:]
    step = pl.program_id(0)
    last = pl.num_programs(0) - 1
    place = lax.axis_index("env")
    states, _, width = site_ref.shape
    block = rows_refs[0].shape[1]
    bonds = mixed.shape[0]
    pairs = pair_ref.shape[0] // bonds
    tall = pair_ref.shape[1] // states

    @pl.when(step == 0)
    def _():
        def group(g, carry):
            base = pl.multiple_of(g * (GROUP * tall), 16)
            parts = []
            for v in range(states):
                term = None
                for r in range(pieces):
                    at = pl.multiple_of(lax.rem(place - r + pieces, pieces) * block, 128)
                    one = jnp.dot(
                        rows_refs[r][pl.ds(base, GROUP * tall), :],
                        site_ref[v, pl.ds(at, block), :],
                        preferred_element_type=jnp.float32,
                    )
                    term = one if term is None else term + one
                parts.append(term * mask_ref[...])
            for i in range(GROUP):
                inner = jnp.concatenate([p[i * tall:(i + 1) * tall] for p in parts], axis=0)
                out = jnp.dot(pair_ref[...], inner.astype(jnp.bfloat16), preferred_element_type=jnp.float32)
                out = out.astype(jnp.bfloat16)
                start = pl.multiple_of((g * GROUP + i) * pairs, 16)
                for k in range(bonds):
                    mixed[k, pl.ds(start, pairs), :] = out[k * pairs:(k + 1) * pairs]
            return carry

        lax.fori_loop(0, mixed.shape[1] // (GROUP * pairs), group, 0)
        total[...] = jnp.zeros_like(total)

    total[...] += lax.dot_general(
        mixed[step], env_ref[0], (((1,), (1,)), ((), ())), preferred_element_type=jnp.float32
    )

    @pl.when(step == last)
    def _():
        out_ref[...] = total[...].astype(out_ref.dtype)


def make_terms(rows_pieces, site, env, pair, mask):
    pieces = len(rows_pieces)
    count, block = rows_pieces[0].shape
    states, depth, width = site.shape
    bonds, outs, _ = env.shape
    tall = bonds * states
    lines = count // tall * states * states
    whole = lambda k: (0, 0)
    return pl.pallas_call(
        functools.partial(apply_kernel, pieces),
        grid=(bonds,),
        in_specs=[pl.BlockSpec((count, block), whole)] * pieces
        + [
            pl.BlockSpec((states, depth, width), lambda k: (0, 0, 0)),
            pl.BlockSpec((1, outs, width), lambda k: (k, 0, 0)),
            pl.BlockSpec(pair.shape, whole),
            pl.BlockSpec(mask.shape, whole),
        ],
        out_specs=pl.BlockSpec((lines, outs), whole),
        out_shape=jax.ShapeDtypeStruct((lines, outs), jnp.bfloat16),
        scratch_shapes=[
            pltpu.VMEM((bonds, lines, width), jnp.bfloat16),
            pltpu.VMEM((lines, outs), jnp.float32),
        ],
        compiler_params=pltpu.CompilerParams(vmem_limit_bytes=VMEM_BYTES),
        cost_estimate=pl.CostEstimate(
            flops=4 * count * depth * states * width + 2 * lines * outs * width * bonds,
            bytes_accessed=2 * (states * depth * width + bonds * outs * width + count * depth + lines * outs),
            transcendentals=0,
        ),
    )(*rows_pieces, site, env, pair, mask)


def hop(value, sections, blocks, sec_step, env_step):
    pairs = [
        (s * blocks + e, (s + sec_step) % sections * blocks + (e + env_step) % blocks)
        for s in range(sections)
        for e in range(blocks)
    ]
    return lax.ppermute(value, ("sec", "env"), pairs)


def body(left_env, left_site, bond_vec, right_site, right_env, mpo, bond_profile, lengths):
    sections, blocks = lax.axis_size("sec"), lax.axis_size("env")
    rows, bonds, width = left_env.shape
    _, states, block = left_site.shape
    sites = mpo.shape[0]
    columns = lax.axis_index("env") * block + jnp.arange(block, dtype=jnp.int32)
    ids = jnp.arange(width, dtype=jnp.int32)

    start = earlier_sites(lengths, sections)
    own = start + lengths[0] - 1
    left_live = bond_profile[(own - 1) % sites]
    middle_live = bond_profile[own % sites]
    out_live = bond_profile[(own + 1) % sites]
    before = (start - 1) % sites
    first = start % sites
    right_live = bond_profile[first]

    left_used = jnp.transpose(left_site, (1, 0, 2))
    live = jnp.stack([left_live, middle_live])
    weights = bond_vec[None, :]

    cuts = [0]
    for share in CHUNK_PARTS:
        cuts.append(cuts[-1] + rows * share // sum(CHUNK_PARTS))
    sent = []
    for low, high in zip(cuts[:-1], cuts[1:]):
        env_rows = left_env[low:high].reshape((high - low) * bonds, width)
        part = make_rows(live, env_rows, left_used, weights)
        sent.append([hop(part, sections, blocks, 1, r) for r in range(blocks)])

    site = jnp.transpose(right_site, (1, 0, 2))
    env = jnp.transpose(right_env, (1, 0, 2))
    mask = (columns < right_live).astype(jnp.float32)[None, :]
    tables = mpo.reshape(sites, -1)
    one = lax.dynamic_index_in_dim(tables, before, 0, False).reshape(bonds, bonds, states, states)
    two = lax.dynamic_index_in_dim(tables, first, 0, False).reshape(bonds, bonds, states, states)
    pair = jnp.einsum("mnsu,nktv->kstvmu", one, two, precision=lax.Precision.HIGHEST)
    pair = pair.reshape(bonds * states * states, -1).astype(jnp.bfloat16)

    keep = (ids < out_live)[None, :]
    results = []
    for pieces in sent:
        terms = make_terms(pieces, site, env, pair, mask)
        back = [hop(terms, sections, blocks, -1, r) for r in range(blocks)]
        total = sum(b.astype(jnp.float32) for b in back)
        results.append(jnp.where(keep, total, 0.0).astype(jnp.bfloat16))
    return jnp.concatenate(results, axis=0).reshape(rows, states, states, width)


def solution(mesh):
    return jax.shard_map(
        body,
        mesh=mesh,
        in_specs=(
            P("sec", None, None),
            P("sec", None, "env"),
            P(("sec", "env")),
            P("sec", None, "env"),
            P("sec", None, "env"),
            P(),
            P(),
            P("sec"),
        ),
        out_specs=P("sec", None, None, None),
        check_vma=False,
    )
```

```python
import functools

import jax
import jax.numpy as jnp
import numpy as np
from jax import lax
from jax.experimental import pallas as pl
from jax.experimental.pallas import tpu as pltpu
from jax.sharding import PartitionSpec as P

CHUNK_PARTS = (1, 2, 1)
GROUP = 8
VMEM_BYTES = 56 * 1024 * 1024


def count_kernel(length_ref, start_ref, slots, send_sem, recv_sem):
    sections = slots.shape[0]
    me = lax.axis_index("sec")
    barrier = pltpu.get_barrier_semaphore()
    for off in range(1, sections):
        pl.semaphore_signal(
            barrier,
            inc=1,
            device_id={"sec": lax.rem(me + off, sections)},
            device_id_type=pl.DeviceIdType.MESH,
        )
    pl.semaphore_wait(barrier, sections - 1)
    copies = []
    for off in range(1, sections):
        copy = pltpu.make_async_remote_copy(
            src_ref=length_ref,
            dst_ref=slots.at[off],
            send_sem=send_sem.at[off],
            recv_sem=recv_sem.at[off],
            device_id={"sec": lax.rem(me + off, sections)},
            device_id_type=pl.DeviceIdType.MESH,
        )
        copy.start()
        copies.append(copy)
    for copy in copies:
        copy.wait()
    total = jnp.zeros_like(start_ref)
    for off in range(1, sections):
        total = total + slots[off] * (me >= off).astype(jnp.int32)
    start_ref[...] = total


def earlier_sites(lengths, sections):
    tile = (8, 128)
    start = pl.pallas_call(
        count_kernel,
        in_specs=[pl.BlockSpec(memory_space=pltpu.VMEM)],
        out_specs=pl.BlockSpec(memory_space=pltpu.VMEM),
        out_shape=jax.ShapeDtypeStruct(tile, jnp.int32),
        scratch_shapes=[
            pltpu.VMEM((sections,) + tile, jnp.int32),
            pltpu.SemaphoreType.DMA((sections,)),
            pltpu.SemaphoreType.DMA((sections,)),
        ],
        compiler_params=pltpu.CompilerParams(collective_id=0, has_side_effects=True),
    )(jnp.broadcast_to(lengths[None, :], tile))
    return start


def row_kernel(start_ref, length_ref, profile_ref, env_ref, site_ref, weight_ref, out_ref, used, held):
    state = pl.program_id(0)
    states = pl.num_programs(0)
    rows, depth = env_ref.shape
    width = weight_ref.shape[1]
    count = out_ref.shape[0] // rows
    sites = profile_ref.shape[0]
    own = start_ref[0, 0] + length_ref[0] - 1 + sites
    left_live = profile_ref[lax.rem(own - 1, sites)]
    middle_live = profile_ref[lax.rem(own, sites)]

    @pl.when(state == 0)
    def _():
        ids = lax.broadcasted_iota(jnp.int32, (1, depth), 1)
        keep = (ids < left_live).astype(jnp.float32).astype(jnp.bfloat16)
        used[...] = env_ref[...] * keep

    ids = lax.axis_index("env") * width + lax.broadcasted_iota(jnp.int32, (1, width), 1)
    scale = jnp.where(ids < middle_live, weight_ref[...], 0.0)
    part = jnp.dot(used[...], site_ref[0], preferred_element_type=jnp.float32) * scale
    for u in range(count):

        @pl.when(state == u)
        def _():
            for at in range(held.shape[0]):
                held[at, pl.ds(u, rows, stride=count), :] = part[:, at * 128:(at + 1) * 128]

    @pl.when(state == states - 1)
    def _():
        for at in range(held.shape[0]):
            out_ref[:, at * 128:(at + 1) * 128] = held[at].astype(out_ref.dtype)


def make_rows(tables, env_rows, left_site, weights):
    rows, depth = env_rows.shape
    states, _, width = left_site.shape
    return pl.pallas_call(
        row_kernel,
        grid=(states,),
        in_specs=[
            pl.BlockSpec(memory_space=pltpu.SMEM),
            pl.BlockSpec(memory_space=pltpu.SMEM),
            pl.BlockSpec(memory_space=pltpu.SMEM),
            pl.BlockSpec((rows, depth), lambda u: (0, 0)),
            pl.BlockSpec((1, depth, width), lambda u: (u, 0, 0)),
            pl.BlockSpec((1, width), lambda u: (0, 0)),
        ],
        out_specs=pl.BlockSpec((rows * states, width), lambda u: (0, 0)),
        out_shape=jax.ShapeDtypeStruct((rows * states, width), jnp.bfloat16),
        scratch_shapes=[
            pltpu.VMEM((rows, depth), jnp.bfloat16),
            pltpu.VMEM((width // 128, rows * states, 128), jnp.float32),
        ],
        compiler_params=pltpu.CompilerParams(vmem_limit_bytes=VMEM_BYTES),
        cost_estimate=pl.CostEstimate(
            flops=2 * rows * states * depth * width,
            bytes_accessed=2 * (rows * depth + states * depth * width + rows * states * width),
            transcendentals=0,
        ),
    )(*tables, env_rows, left_site, weights)


def apply_kernel(pieces, *refs):
    rows_refs = refs[:pieces]
    start_ref, profile_ref, site_ref, env_ref, pair_ref, out_ref, mixed, total = refs[pieces:]
    step = pl.program_id(0)
    last = pl.num_programs(0) - 1
    place = lax.axis_index("env")
    states, _, width = site_ref.shape
    block = rows_refs[0].shape[1]
    bonds = mixed.shape[0]
    pairs = pair_ref.shape[0] // bonds
    tall = pair_ref.shape[1] // states

    @pl.when(step == 0)
    def _():
        right_live = profile_ref[lax.rem(start_ref[0, 0], profile_ref.shape[0])]
        ids = place * width + lax.broadcasted_iota(jnp.int32, (1, width), 1)
        keep = (ids < right_live).astype(jnp.float32)

        def group(g, carry):
            base = pl.multiple_of(g * (GROUP * tall), 16)
            parts = []
            for v in range(states):
                term = None
                for r in range(pieces):
                    at = pl.multiple_of(lax.rem(place - r + pieces, pieces) * block, 128)
                    one = jnp.dot(
                        rows_refs[r][pl.ds(base, GROUP * tall), :],
                        site_ref[v, pl.ds(at, block), :],
                        preferred_element_type=jnp.float32,
                    )
                    term = one if term is None else term + one
                parts.append(term * keep)
            for i in range(GROUP):
                inner = jnp.concatenate([p[i * tall:(i + 1) * tall] for p in parts], axis=0)
                out = jnp.dot(pair_ref[...], inner.astype(jnp.bfloat16), preferred_element_type=jnp.float32)
                out = out.astype(jnp.bfloat16)
                start = pl.multiple_of((g * GROUP + i) * pairs, 16)
                for k in range(bonds):
                    mixed[k, pl.ds(start, pairs), :] = out[k * pairs:(k + 1) * pairs]
            return carry

        lax.fori_loop(0, mixed.shape[1] // (GROUP * pairs), group, 0)
        total[...] = jnp.zeros_like(total)

    total[...] += lax.dot_general(
        mixed[step], env_ref[0], (((1,), (1,)), ((), ())), preferred_element_type=jnp.float32
    )

    @pl.when(step == last)
    def _():
        out_ref[...] = total[...].astype(out_ref.dtype)


def make_terms(rows_pieces, start, profile, site, env, pair):
    pieces = len(rows_pieces)
    count, block = rows_pieces[0].shape
    states, depth, width = site.shape
    bonds, outs, _ = env.shape
    tall = bonds * states
    lines = count // tall * states * states
    whole = lambda k: (0, 0)
    return pl.pallas_call(
        functools.partial(apply_kernel, pieces),
        grid=(bonds,),
        in_specs=[pl.BlockSpec((count, block), whole)] * pieces
        + [
            pl.BlockSpec(memory_space=pltpu.SMEM),
            pl.BlockSpec(memory_space=pltpu.SMEM),
            pl.BlockSpec((states, depth, width), lambda k: (0, 0, 0)),
            pl.BlockSpec((1, outs, width), lambda k: (k, 0, 0)),
            pl.BlockSpec(pair.shape, whole),
        ],
        out_specs=pl.BlockSpec((lines, outs), whole),
        out_shape=jax.ShapeDtypeStruct((lines, outs), jnp.bfloat16),
        scratch_shapes=[
            pltpu.VMEM((bonds, lines, width), jnp.bfloat16),
            pltpu.VMEM((lines, outs), jnp.float32),
        ],
        compiler_params=pltpu.CompilerParams(vmem_limit_bytes=VMEM_BYTES),
        cost_estimate=pl.CostEstimate(
            flops=4 * count * depth * states * width + 2 * lines * outs * width * bonds,
            bytes_accessed=2 * (states * depth * width + bonds * outs * width + count * depth + lines * outs),
            transcendentals=0,
        ),
    )(*rows_pieces, start, profile, site, env, pair)


def pair_kernel(one_ref, two_ref, rows_ref, match_ref, columns_ref, out_ref):
    product = lax.dot_general(
        two_ref[...],
        one_ref[...],
        (((0,), (0,)), ((), ())),
        precision=lax.Precision.HIGHEST,
        preferred_element_type=jnp.float32,
    ).astype(jnp.bfloat16)
    total = jnp.zeros(out_ref.shape, jnp.float32)
    for v in range(rows_ref.shape[0]):
        picked = jnp.dot(rows_ref[v], product, preferred_element_type=jnp.float32)
        picked = (picked * match_ref[...]).astype(jnp.bfloat16)
        total = total + jnp.dot(picked, columns_ref[v], preferred_element_type=jnp.float32)
    out_ref[...] = total.astype(out_ref.dtype)


def make_pair(one, two, bonds, states):
    size = bonds * states * states
    at = np.arange(size)
    outer, middle, inner = at // (states * states), at // states % states, at % states
    picks, places = [], []
    for v in range(states):
        picks.append(((outer * states + inner) * states + v)[:, None] == at[None, :])
        places.append((v * bonds * states + outer * states + inner)[:, None] == at[None, :])
    return pl.pallas_call(
        pair_kernel,
        out_shape=jax.ShapeDtypeStruct((size, size), jnp.bfloat16),
        compiler_params=pltpu.CompilerParams(vmem_limit_bytes=VMEM_BYTES),
    )(
        one,
        two,
        jnp.asarray(np.stack(picks), jnp.bfloat16),
        jnp.asarray(middle[:, None] == middle[None, :], jnp.float32),
        jnp.asarray(np.stack(places), jnp.bfloat16),
    )


def hop(value, sections, blocks, sec_step, env_step):
    pairs = [
        (s * blocks + e, (s + sec_step) % sections * blocks + (e + env_step) % blocks)
        for s in range(sections)
        for e in range(blocks)
    ]
    return lax.ppermute(value, ("sec", "env"), pairs)


def body(left_env, left_site, bond_vec, right_site, right_env, mpo, bond_profile, lengths):
    sections, blocks = lax.axis_size("sec"), lax.axis_size("env")
    rows, bonds, width = left_env.shape
    _, states, block = left_site.shape
    sites = mpo.shape[0]
    ids = jnp.arange(width, dtype=jnp.int32)

    start = earlier_sites(lengths, sections)
    left_used = jnp.transpose(left_site, (1, 0, 2))
    small = (start, lengths, bond_profile)
    weights = bond_vec[None, :]

    cuts = [0]
    for share in CHUNK_PARTS:
        cuts.append(cuts[-1] + rows * share // sum(CHUNK_PARTS))
    sent = []
    for low, high in zip(cuts[:-1], cuts[1:]):
        env_rows = left_env[low:high].reshape((high - low) * bonds, width)
        part = make_rows(small, env_rows, left_used, weights)
        sent.append([hop(part, sections, blocks, 1, r) for r in range(blocks)])

    site = jnp.transpose(right_site, (1, 0, 2))
    env = jnp.transpose(right_env, (1, 0, 2))
    origin = start[0, 0]
    out_live = bond_profile[(origin + lengths[0]) % sites]
    one = lax.dynamic_index_in_dim(mpo, (origin - 1) % sites, 0, False)
    one = one.reshape(bonds, bonds, states * states).transpose(1, 0, 2).reshape(bonds, -1)
    two = lax.dynamic_index_in_dim(mpo, origin % sites, 0, False).reshape(bonds, -1)
    pair = make_pair(one, two, bonds, states)

    keep = (ids < out_live)[None, :]
    results = []
    for pieces in sent:
        terms = make_terms(pieces, start, bond_profile, site, env, pair)
        back = [hop(terms, sections, blocks, -1, r) for r in range(blocks)]
        total = sum(b.astype(jnp.float32) for b in back)
        results.append(jnp.where(keep, total, 0.0).astype(jnp.bfloat16))
    return jnp.concatenate(results, axis=0).reshape(rows, states, states, width)


def solution(mesh):
    return jax.shard_map(
        body,
        mesh=mesh,
        in_specs=(
            P("sec", None, None),
            P("sec", None, "env"),
            P(("sec", "env")),
            P("sec", None, "env"),
            P("sec", None, "env"),
            P(),
            P(),
            P("sec"),
        ),
        out_specs=P("sec", None, None, None),
        check_vma=False,
    )
```

```python
import functools

import jax
import jax.numpy as jnp
import numpy as np
from jax import lax
from jax.experimental import pallas as pl
from jax.experimental.pallas import tpu as pltpu
from jax.sharding import PartitionSpec as P

CHUNK_PARTS = (1, 2, 1)
GROUP = 8
VMEM_BYTES = 56 * 1024 * 1024


def count_kernel(length_ref, start_ref, slots, send_sem, recv_sem):
    sections = slots.shape[0]
    me = lax.axis_index("sec")
    barrier = pltpu.get_barrier_semaphore()
    for off in range(1, sections):
        pl.semaphore_signal(
            barrier,
            inc=1,
            device_id={"sec": lax.rem(me + off, sections)},
            device_id_type=pl.DeviceIdType.MESH,
        )
    pl.semaphore_wait(barrier, sections - 1)
    copies = []
    for off in range(1, sections):
        copy = pltpu.make_async_remote_copy(
            src_ref=length_ref,
            dst_ref=slots.at[off],
            send_sem=send_sem.at[off],
            recv_sem=recv_sem.at[off],
            device_id={"sec": lax.rem(me + off, sections)},
            device_id_type=pl.DeviceIdType.MESH,
        )
        copy.start()
        copies.append(copy)
    for copy in copies:
        copy.wait()
    total = jnp.zeros_like(start_ref)
    for off in range(1, sections):
        total = total + slots[off] * (me >= off).astype(jnp.int32)
    start_ref[...] = total


def earlier_sites(lengths, sections):
    tile = (8, 128)
    start = pl.pallas_call(
        count_kernel,
        in_specs=[pl.BlockSpec(memory_space=pltpu.VMEM)],
        out_specs=pl.BlockSpec(memory_space=pltpu.VMEM),
        out_shape=jax.ShapeDtypeStruct(tile, jnp.int32),
        scratch_shapes=[
            pltpu.VMEM((sections,) + tile, jnp.int32),
            pltpu.SemaphoreType.DMA((sections,)),
            pltpu.SemaphoreType.DMA((sections,)),
        ],
        compiler_params=pltpu.CompilerParams(collective_id=0, has_side_effects=True),
    )(jnp.broadcast_to(lengths[None, :], tile))
    return start


def row_kernel(start_ref, length_ref, profile_ref, env_ref, site_ref, weight_ref, out_ref, used, held):
    state = pl.program_id(0)
    states = pl.num_programs(0)
    rows, depth = env_ref.shape
    width = weight_ref.shape[1]
    count = out_ref.shape[0] // rows
    sites = profile_ref.shape[0]
    own = start_ref[0, 0] + length_ref[0] - 1 + sites
    left_live = profile_ref[lax.rem(own - 1, sites)]
    middle_live = profile_ref[lax.rem(own, sites)]

    @pl.when(state == 0)
    def _():
        ids = lax.broadcasted_iota(jnp.int32, (1, depth), 1)
        keep = (ids < left_live).astype(jnp.float32).astype(jnp.bfloat16)
        used[...] = env_ref[...] * keep

    ids = lax.axis_index("env") * width + lax.broadcasted_iota(jnp.int32, (1, width), 1)
    scale = jnp.where(ids < middle_live, weight_ref[...], 0.0)
    part = jnp.dot(used[...], site_ref[0], preferred_element_type=jnp.float32) * scale
    for u in range(count):

        @pl.when(state == u)
        def _():
            for at in range(held.shape[0]):
                held[at, pl.ds(u, rows, stride=count), :] = part[:, at * 128:(at + 1) * 128]

    @pl.when(state == states - 1)
    def _():
        for at in range(held.shape[0]):
            out_ref[:, at * 128:(at + 1) * 128] = held[at].astype(out_ref.dtype)


def make_rows(tables, env_rows, left_site, weights):
    rows, depth = env_rows.shape
    states, _, width = left_site.shape
    return pl.pallas_call(
        row_kernel,
        grid=(states,),
        in_specs=[
            pl.BlockSpec(memory_space=pltpu.SMEM),
            pl.BlockSpec(memory_space=pltpu.SMEM),
            pl.BlockSpec(memory_space=pltpu.SMEM),
            pl.BlockSpec((rows, depth), lambda u: (0, 0)),
            pl.BlockSpec((1, depth, width), lambda u: (u, 0, 0)),
            pl.BlockSpec((1, width), lambda u: (0, 0)),
        ],
        out_specs=pl.BlockSpec((rows * states, width), lambda u: (0, 0)),
        out_shape=jax.ShapeDtypeStruct((rows * states, width), jnp.bfloat16),
        scratch_shapes=[
            pltpu.VMEM((rows, depth), jnp.bfloat16),
            pltpu.VMEM((width // 128, rows * states, 128), jnp.float32),
        ],
        compiler_params=pltpu.CompilerParams(vmem_limit_bytes=VMEM_BYTES),
        cost_estimate=pl.CostEstimate(
            flops=2 * rows * states * depth * width,
            bytes_accessed=2 * (rows * depth + states * depth * width + rows * states * width),
            transcendentals=0,
        ),
    )(*tables, env_rows, left_site, weights)


def apply_kernel(pieces, *refs):
    rows_refs = refs[:pieces]
    start_ref, profile_ref, site_ref, env_ref, pair_ref, out_ref, mixed, total, env_held, env_sem = refs[pieces:]
    env_copy = pltpu.make_async_copy(env_ref, env_held, env_sem)
    env_copy.start()
    place = lax.axis_index("env")
    states, _, width = site_ref.shape
    block = rows_refs[0].shape[1]
    bonds = mixed.shape[0]
    pairs = pair_ref.shape[0] // bonds
    tall = pair_ref.shape[1] // states

    right_live = profile_ref[lax.rem(start_ref[0, 0], profile_ref.shape[0])]
    ids = place * width + lax.broadcasted_iota(jnp.int32, (1, width), 1)
    keep = (ids < right_live).astype(jnp.float32)

    def group(g, carry):
        base = pl.multiple_of(g * (GROUP * tall), 16)
        parts = []
        for v in range(states):
            term = None
            for r in range(pieces):
                at = pl.multiple_of(lax.rem(place - r + pieces, pieces) * block, 128)
                one = jnp.dot(
                    rows_refs[r][pl.ds(base, GROUP * tall), :],
                    site_ref[v, pl.ds(at, block), :],
                    preferred_element_type=jnp.float32,
                )
                term = one if term is None else term + one
            parts.append(term * keep)
        for i in range(GROUP):
            inner = jnp.concatenate([p[i * tall:(i + 1) * tall] for p in parts], axis=0)
            out = jnp.dot(pair_ref[...], inner.astype(jnp.bfloat16), preferred_element_type=jnp.float32)
            out = out.astype(jnp.bfloat16)
            start = pl.multiple_of((g * GROUP + i) * pairs, 16)
            for k in range(bonds):
                mixed[k, pl.ds(start, pairs), :] = out[k * pairs:(k + 1) * pairs]
        return carry

    lax.fori_loop(0, mixed.shape[1] // (GROUP * pairs), group, 0)
    total[...] = jnp.zeros_like(total)
    env_copy.wait()

    def bond(k, carry):
        total[...] += lax.dot_general(
            mixed[k], env_held[k], (((1,), (1,)), ((), ())), preferred_element_type=jnp.float32
        )
        return carry

    lax.fori_loop(0, bonds, bond, 0)
    out_ref[...] = total[...].astype(out_ref.dtype)


def make_terms(rows_pieces, start, profile, site, env, pair):
    pieces = len(rows_pieces)
    count, block = rows_pieces[0].shape
    states, depth, width = site.shape
    bonds, outs, _ = env.shape
    tall = bonds * states
    lines = count // tall * states * states
    near = pl.BlockSpec(memory_space=pltpu.VMEM)
    table = pl.BlockSpec(memory_space=pltpu.SMEM)
    return pl.pallas_call(
        functools.partial(apply_kernel, pieces),
        in_specs=[near] * pieces + [table, table, near, pl.BlockSpec(memory_space=pl.ANY), near],
        out_specs=near,
        out_shape=jax.ShapeDtypeStruct((lines, outs), jnp.bfloat16),
        scratch_shapes=[
            pltpu.VMEM((bonds, lines, width), jnp.bfloat16),
            pltpu.VMEM((lines, outs), jnp.float32),
            pltpu.VMEM(env.shape, jnp.bfloat16),
            pltpu.SemaphoreType.DMA,
        ],
        compiler_params=pltpu.CompilerParams(vmem_limit_bytes=VMEM_BYTES),
        cost_estimate=pl.CostEstimate(
            flops=4 * count * depth * states * width + 2 * lines * outs * width * bonds,
            bytes_accessed=2 * (states * depth * width + bonds * outs * width + count * depth + lines * outs),
            transcendentals=0,
        ),
    )(*rows_pieces, start, profile, site, env, pair)


def pair_kernel(one_ref, two_ref, rows_ref, match_ref, columns_ref, out_ref):
    product = lax.dot_general(
        two_ref[...],
        one_ref[...],
        (((0,), (0,)), ((), ())),
        precision=lax.Precision.HIGHEST,
        preferred_element_type=jnp.float32,
    ).astype(jnp.bfloat16)
    total = jnp.zeros(out_ref.shape, jnp.float32)
    for v in range(rows_ref.shape[0]):
        picked = jnp.dot(rows_ref[v], product, preferred_element_type=jnp.float32)
        picked = (picked * match_ref[...]).astype(jnp.bfloat16)
        total = total + jnp.dot(picked, columns_ref[v], preferred_element_type=jnp.float32)
    out_ref[...] = total.astype(out_ref.dtype)


def make_pair(one, two, bonds, states):
    size = bonds * states * states
    at = np.arange(size)
    outer, middle, inner = at // (states * states), at // states % states, at % states
    picks, places = [], []
    for v in range(states):
        picks.append(((outer * states + inner) * states + v)[:, None] == at[None, :])
        places.append((v * bonds * states + outer * states + inner)[:, None] == at[None, :])
    return pl.pallas_call(
        pair_kernel,
        out_shape=jax.ShapeDtypeStruct((size, size), jnp.bfloat16),
        compiler_params=pltpu.CompilerParams(vmem_limit_bytes=VMEM_BYTES),
    )(
        one,
        two,
        jnp.asarray(np.stack(picks), jnp.bfloat16),
        jnp.asarray(middle[:, None] == middle[None, :], jnp.float32),
        jnp.asarray(np.stack(places), jnp.bfloat16),
    )


def hop(value, sections, blocks, sec_step, env_step):
    pairs = [
        (s * blocks + e, (s + sec_step) % sections * blocks + (e + env_step) % blocks)
        for s in range(sections)
        for e in range(blocks)
    ]
    return lax.ppermute(value, ("sec", "env"), pairs)


def body(left_env, left_site, bond_vec, right_site, right_env, mpo, bond_profile, lengths):
    sections, blocks = lax.axis_size("sec"), lax.axis_size("env")
    rows, bonds, width = left_env.shape
    _, states, block = left_site.shape
    sites = mpo.shape[0]
    ids = jnp.arange(width, dtype=jnp.int32)

    start = earlier_sites(lengths, sections)
    left_used = jnp.transpose(left_site, (1, 0, 2))
    small = (start, lengths, bond_profile)
    weights = bond_vec[None, :]

    cuts = [0]
    for share in CHUNK_PARTS:
        cuts.append(cuts[-1] + rows * share // sum(CHUNK_PARTS))
    sent = []
    for low, high in zip(cuts[:-1], cuts[1:]):
        env_rows = left_env[low:high].reshape((high - low) * bonds, width)
        part = make_rows(small, env_rows, left_used, weights)
        sent.append([hop(part, sections, blocks, 1, r) for r in range(blocks)])

    site = jnp.transpose(right_site, (1, 0, 2))
    env = jnp.transpose(right_env, (1, 0, 2))
    origin = start[0, 0]
    out_live = bond_profile[(origin + lengths[0]) % sites]
    one = lax.dynamic_index_in_dim(mpo, (origin - 1) % sites, 0, False)
    one = one.reshape(bonds, bonds, states * states).transpose(1, 0, 2).reshape(bonds, -1)
    two = lax.dynamic_index_in_dim(mpo, origin % sites, 0, False).reshape(bonds, -1)
    pair = make_pair(one, two, bonds, states)

    keep = (ids < out_live)[None, :]
    results = []
    for pieces in sent:
        terms = make_terms(pieces, start, bond_profile, site, env, pair)
        back = [hop(terms, sections, blocks, -1, r) for r in range(blocks)]
        total = sum(b.astype(jnp.float32) for b in back)
        results.append(jnp.where(keep, total, 0.0).astype(jnp.bfloat16))
    return jnp.concatenate(results, axis=0).reshape(rows, states, states, width)


def solution(mesh):
    return jax.shard_map(
        body,
        mesh=mesh,
        in_specs=(
            P("sec", None, None),
            P("sec", None, "env"),
            P(("sec", "env")),
            P("sec", None, "env"),
            P("sec", None, "env"),
            P(),
            P(),
            P("sec"),
        ),
        out_specs=P("sec", None, None, None),
        check_vma=False,
    )
```
